32 devices in a mesh: clips: 2 (over x), leaf: 16 (over z, y, core).
Axes of the slice: x: 2, y: 2, z: 4, core: 2. Of those that a mesh axis runs over, the one named last changes fastest.
Arguments:
- points: bfloat16 [131072, 64], P(('clips', 'leaf')), parts along dimension 0, may hold values from -6 to 6
- charges: bfloat16 [131072, 16], P(('clips', 'leaf')), parts along dimension 0, may hold values from -6 to 6
- near_list: int32 [256, 15], P(('clips', 'leaf')), parts along dimension 0, may hold values from 0 to 127, as said below
- near_count: int32 [256], P(('clips', 'leaf')), parts along dimension 0, may hold values from 1 to 15
- skel_index: int32 [32, 256], P(('clips', 'leaf')), parts along dimension 0, may hold values from 0 to 4095, as said below
- basis: bfloat16 [131072, 256], P(('clips', 'leaf')), parts along dimension 0, may hold values from -0.375 to 0.375
- upper_index: int32 [32, 2, 256], P(('clips', 'leaf')), parts along dimension 0, may hold values from 0 to 511, as said below
- upper_basis: bfloat16 [32, 2, 512, 256], P(('clips', 'leaf')), parts along dimension 0, as said below
- far_list: int32 [32, 2, 3], P(('clips', 'leaf')), parts along dimension 0, may hold values from -1 to 15, as said below
Outputs:
- product: float32 [131072, 16], P(('clips', 'leaf')), parts along dimension 0
The draws below stay inside these ranges and needn't reach their ends.
There are 2 independent parts, one for each index of `clips`. The reference program is written for one: setup_inputs(seed, part) draws one part's arguments, and reference() takes and returns one part's arrays. A program takes and returns all parts, laid end to end along the dimension named above; each array names one. Nothing has to cross between parts.
Inputs may be any that keep to these rules, and one draw needn't show every extreme that they name: For s < near_count[a], near_list[a, s] are distinct leaves within 7 of a in increasing order, a among them; b is in a's list exactly when a is in b's; later slots hold a. `skel_index`: entry i lies in [i * 16, (i + 1) * 16). `upper_index`: entry i of a level is 2i or 2i + 1; rows of the devices of one node are equal. `upper_basis`: rows of the devices of one node are equal. `far_list`: entries of node j at level l are -1 or distinct nodes of that level among j - 3, j - 2, j + 2, j + 3 that are not children of the parent's non-neighbours (for even j: j - 2, j + 2, j + 3; for odd j: j - 3, j - 2, j + 2); rows of the devices of one node are equal.
All inputs are finite; a program needn't handle non-finite values.
Results may differ from the reference program's by a relative error of at most 0.0053.
Values may be sent and summed in bfloat16 or wider, within the bound.
No kernel may reach another device: no remote copies, remote signals or barrier semaphores. Data moves between devices by JAX's collectives and lax.ppermute only.
A program may use at most 64 MiB of HBM per device.

```python
import jax
import jax.numpy as jnp
from jax import lax

DIM = 64
RHS = 16
LEAF = 512
S = 256
REACH = 7
FAR = 3
LEVELS = 3
POINTS_DEV = 4096
NLEAVES = 128
POINTS = 65536
N_LEAF = 16


def near_graph(key):
    total = NLEAVES
    base = jnp.arange(total, dtype=jnp.int32)[:, None]
    dist = jnp.arange(1, REACH + 1, dtype=jnp.int32)[None, :]
    bits = jax.random.randint(jax.random.fold_in(key, 11), (total, REACH), 0, 8) < 3
    star = jax.random.randint(jax.random.fold_in(key, 12), (), REACH, total - REACH)
    link = (bits | (base == star) | (base + dist == star)) & (base + dist < total)
    padded = jnp.concatenate([jnp.zeros((REACH, REACH), bool), link], axis=0)
    rows_back = base - dist + REACH
    cols = jnp.broadcast_to(dist - 1, (total, REACH))
    lower = padded[rows_back, cols]
    used = jnp.concatenate([lower[:, ::-1], jnp.ones((total, 1), bool), link], axis=1)
    offsets = jnp.arange(-REACH, REACH + 1, dtype=jnp.int32)
    count = jnp.sum(used.astype(jnp.int32), axis=1).astype(jnp.int32)
    score = jnp.where(used, offsets[None, :], offsets[None, :] + 4 * REACH + 4)
    order = jnp.argsort(score, axis=1)
    chosen = offsets[order]
    slots = jnp.arange(2 * REACH + 1, dtype=jnp.int32)
    listed = jnp.where(slots[None, :] < count[:, None], base + chosen, base)
    return (listed.astype(jnp.int32), count)


def draw_near_list(key, part):
    shared = near_graph(key)
    return shared[0]


def draw_near_count(key, part):
    shared = near_graph(key)
    return shared[1]


def draw_skel_index(key, part):
    key = jax.random.fold_in(key, 3)
    block = POINTS_DEV // S
    offsets = jax.random.randint(key, (N_LEAF, S), 0, block)
    column = jnp.arange(S, dtype=jnp.int32)[None, :]
    picks = column * block + offsets
    picks = jnp.where(column == 0, 0, picks)
    picks = jnp.where(column == S - 1, POINTS_DEV - 1, picks)
    return picks.astype(jnp.int32)


def draw_upper_index(key, part):
    key = jax.random.fold_in(key, 4)
    levels = []
    column = jnp.arange(S, dtype=jnp.int32)[None, :]
    for level in range(1, LEVELS):
        stride = 2 ** level
        halves = jax.random.randint(jax.random.fold_in(key, level), (N_LEAF // stride, S), 0, 2)
        picks = 2 * column + halves
        picks = jnp.where(column == 0, 0, picks)
        picks = jnp.where(column == S - 1, 2 * S - 1, picks)
        levels.append(jnp.repeat(picks, stride, axis=0))
    return jnp.stack(levels, axis=1).astype(jnp.int32)


def draw_upper_basis(key, part):
    key = jax.random.fold_in(key, 5)
    levels = []
    for level in range(1, LEVELS):
        stride = 2 ** level
        values = jax.random.normal(jax.random.fold_in(key, level), (N_LEAF // stride, 2 * S, S), jnp.float32)
        values = values * (2.0 * S) ** (-0.5)
        levels.append(jnp.repeat(values, stride, axis=0))
    return jnp.stack(levels, axis=1).astype(jnp.bfloat16)


def draw_far_list(key, part):
    key = jax.random.fold_in(key, 6)
    levels = []
    for level in range(LEVELS - 1):
        stride = 2 ** level
        nodes = N_LEAF // stride
        index = jnp.arange(nodes, dtype=jnp.int32)[:, None]
        even = index % 2 == 0
        steps_even = jnp.array([[-2, 2, 3]], dtype=jnp.int32)
        steps_odd = jnp.array([[-3, -2, 2]], dtype=jnp.int32)
        cand = index + jnp.where(even, steps_even, steps_odd)
        keep = jax.random.randint(jax.random.fold_in(key, level), (nodes, FAR), 0, 4) > 0
        valid = (cand >= 0) & (cand < nodes) & keep
        listed = jnp.where(valid, cand, -1)
        levels.append(jnp.repeat(listed, stride, axis=0))
    return jnp.stack(levels, axis=1).astype(jnp.int32)


def block_levels(stream_key, shape, pieces, least, top_value):
    level = 1.0
    for axis_at, shards_of in pieces:
        heights = jax.random.uniform(jax.random.fold_in(jax.random.fold_in(stream_key, 6), axis_at), (shards_of,), jnp.float32, least / len(pieces), top_value / len(pieces))
        level = level * jnp.repeat(jnp.exp(heights), shape[axis_at] // shards_of).reshape((-1,) + (1,) * (len(shape) - 1 - axis_at))
    return level


def scatter_about(rng, shape, deviation, bound, cuts=(), kind=jnp.bfloat16):
    gain = block_levels(rng, shape, cuts, -0.22, 0.18) if cuts else 1.0
    values = jax.random.normal(rng, shape, jnp.float32) * deviation * gain
    return jnp.minimum(jnp.maximum(values, -bound), bound).astype(kind)


def setup_inputs(seed: int = 0, part: int = 0) -> dict:
    key_of = jax.random.split(jax.random.key(seed), 10)
    part_splits = jax.random.split(jax.random.fold_in(key_of[9], part), 10)
    return {
        "points": scatter_about(part_splits[0], (POINTS, DIM), 1.0, 6.0, ((0, 16),)),
        "charges": scatter_about(part_splits[1], (POINTS, RHS), 1.0, 6.0, ((0, 16),)),
        "near_list": draw_near_list(jax.random.fold_in(jax.random.fold_in(key_of[9], part), 71), part),
        "near_count": draw_near_count(jax.random.fold_in(jax.random.fold_in(key_of[9], part), 71), part),
        "skel_index": draw_skel_index(jax.random.fold_in(jax.random.fold_in(key_of[9], part), 71), part),
        "basis": scatter_about(part_splits[5], (POINTS, S), S ** -0.5, 0.375, ((0, 16),)),
        "upper_index": draw_upper_index(jax.random.fold_in(jax.random.fold_in(key_of[9], part), 71), part),
        "upper_basis": draw_upper_basis(jax.random.fold_in(jax.random.fold_in(key_of[9], part), 71), part),
        "far_list": draw_far_list(jax.random.fold_in(jax.random.fold_in(key_of[9], part), 71), part),
    }


def kernel_tile(left, right, spread):
    left_f = left.astype(jnp.float32)
    right_f = right.astype(jnp.float32)
    left_sq = jnp.sum(left_f * left_f, axis=1)
    right_sq = jnp.sum(right_f * right_f, axis=1)
    cross = lax.dot_general(left, right, (((1,), (1,)), ((), ())), preferred_element_type=jnp.float32)
    dist = left_sq[:, None] + right_sq[None, :] - 2.0 * cross
    return jnp.exp(-dist / spread).astype(jnp.bfloat16)


def reference(points, charges, near_list, near_count, skel_index, basis, upper_index, upper_basis, far_list):
    spread = 0.5 * DIM
    leaf_pts = points.reshape(NLEAVES, LEAF, DIM)
    leaf_w = charges.reshape(NLEAVES, LEAF, RHS)

    def one_leaf(own):
        def step(slot, acc):
            other = near_list[own, slot]
            tile = kernel_tile(leaf_pts[own], leaf_pts[other], spread)
            return acc + jnp.dot(tile, leaf_w[other], preferred_element_type=jnp.float32)
        return lax.fori_loop(0, near_count[own], step, jnp.zeros((LEAF, RHS), jnp.float32))

    near = lax.map(one_leaf, jnp.arange(NLEAVES, dtype=jnp.int32)).reshape(POINTS, RHS)

    devices = N_LEAF
    dev_pts = points.reshape(devices, POINTS_DEV, DIM)
    skel_pts = jnp.take_along_axis(dev_pts, skel_index.astype(jnp.int32)[:, :, None], axis=1)
    skel_w = jnp.einsum("gps,gpr->gsr", basis.reshape(devices, POINTS_DEV, S).astype(jnp.float32),
                        charges.reshape(devices, POINTS_DEV, RHS).astype(jnp.float32)).astype(jnp.bfloat16)
    all_pts = [skel_pts]
    all_w = [skel_w]
    for level in range(1, LEVELS):
        stride = 2 ** level
        nodes = devices // stride
        joined_pts = all_pts[-1].reshape(nodes, 2 * S, DIM)
        joined_w = all_w[-1].reshape(nodes, 2 * S, RHS)
        picks = upper_index[::stride, level - 1].astype(jnp.int32)
        mats = upper_basis[::stride, level - 1]
        all_pts.append(jnp.take_along_axis(joined_pts, picks[:, :, None], axis=1))
        all_w.append(jnp.einsum("nks,nkr->nsr", mats.astype(jnp.float32), joined_w.astype(jnp.float32)).astype(jnp.bfloat16))

    potentials = []
    for level in range(LEVELS - 1):
        stride = 2 ** level
        lists = far_list[::stride, level]
        level_pts = all_pts[level]
        level_w = all_w[level]

        def node_term(item):
            own_pts, row = item
            total = jnp.zeros((S, RHS), jnp.float32)
            for slot in range(FAR):
                other = row[slot]
                safe = jnp.maximum(other, 0)
                tile = kernel_tile(own_pts, level_pts[safe], spread)
                term = jnp.dot(tile, level_w[safe], preferred_element_type=jnp.float32)
                total = total + jnp.where(other >= 0, term, jnp.zeros_like(term))
            return total

        potentials.append(lax.map(node_term, (level_pts, lists)))

    top_nodes = devices // 2 ** (LEVELS - 1)
    flat_pts = all_pts[-1].reshape(top_nodes * S, DIM)
    flat_w = all_w[-1].reshape(top_nodes * S, RHS)
    owner = jnp.arange(top_nodes * S, dtype=jnp.int32) // S

    def top_term(item):
        own_pts, node = item
        tile = kernel_tile(own_pts, flat_pts, spread)
        tile = jnp.where((jnp.abs(owner - node) >= 2)[None, :], tile, jnp.zeros_like(tile))
        return jnp.dot(tile, flat_w, preferred_element_type=jnp.float32)

    field = lax.map(top_term, (all_pts[-1], jnp.arange(top_nodes, dtype=jnp.int32)))
    for level in range(LEVELS - 1, 0, -1):
        stride = 2 ** level
        nodes = devices // stride
        mats = upper_basis[::stride, level - 1]
        spread_down = jnp.einsum("nks,nsr->nkr", mats.astype(jnp.float32),
                                 field.astype(jnp.bfloat16).astype(jnp.float32))
        field = potentials[level - 1] + spread_down.reshape(nodes * 2, S, RHS)
    far = jnp.einsum("gps,gsr->gpr", basis.reshape(devices, POINTS_DEV, S).astype(jnp.float32),
                     field.astype(jnp.bfloat16).astype(jnp.float32)).reshape(POINTS, RHS)
    return near + far
```

```python
import jax
import jax.numpy as jnp
from jax import lax
from jax.experimental import pallas as pl
from jax.experimental.pallas import tpu as pltpu
from jax.sharding import PartitionSpec as P

LEAF = 512
GROUP = 4
UNROLL = 4
EXTRA = 16
VMEM = pl.BlockSpec(memory_space=pltpu.VMEM)
SMEM = pl.BlockSpec(memory_space=pltpu.SMEM)
LIMIT = 48 << 20
F32 = jnp.float32
BF16 = jnp.bfloat16


def dot(left, right):
    return jnp.dot(left, right, preferred_element_type=F32)


def dot_nt(left, right):
    return lax.dot_general(left, right, (((1,), (1,)), ((), ())), preferred_element_type=F32)


def dot_tn(left, right):
    return lax.dot_general(left, right, (((0,), (0,)), ((), ())), preferred_element_type=F32)


def norm_rows(feats, spread, ones_first):
    norm = jnp.sum(feats * feats, axis=0, keepdims=True) * (-1.0 / spread)
    high = norm.astype(BF16).astype(F32)
    mid = (norm - high).astype(BF16).astype(F32)
    low = norm - high - mid
    row = lax.broadcasted_iota(jnp.int32, (EXTRA, feats.shape[1]), 0)
    start = 3 if ones_first else 0
    rows = jnp.where((row >= 3 - start) & (row < 6 - start), 1.0, 0.0)
    for at, piece in enumerate((high, mid, low)):
        rows = jnp.where(row == start + at, piece, rows)
    return rows.astype(BF16)


def source_side(feats, spread):
    return jnp.concatenate([feats, norm_rows(feats.astype(F32), spread, False)], axis=0)


def target_side(feats, spread):
    feats_f = feats.astype(F32)
    scaled = (feats_f * (2.0 / spread)).astype(BF16)
    return jnp.concatenate([scaled, norm_rows(feats_f, spread, True)], axis=0)


def padded(rows, height):
    gap = height - rows.shape[0]
    return jnp.concatenate([rows, jnp.zeros((gap, rows.shape[1]), rows.dtype)], axis=0)


def one_hot(index, height, offset):
    rows = lax.broadcasted_iota(jnp.int32, (height, index.shape[1]), 0) + offset
    return jnp.where(rows == index, 1.0, 0.0).astype(BF16)


def upward_kernel(pts, w, basis, skel, upper, ubasis, out, own, block):
    me = lax.axis_index("leaf")
    side = lax.rem(me, 2)
    child = lax.rem(me // 2, 2)
    feats, rows = pts.shape
    rhs = w.shape[0]
    skeleton = basis.shape[1]
    half = rows // 2
    lanes = skeleton // 2
    picks = [
        dot(
            pts[:, at * half : (at + 1) * half],
            one_hot(skel[:, at * lanes : (at + 1) * lanes], half, at * half),
        )
        for at in range(2)
    ]
    pts0 = jnp.concatenate(picks, axis=1).astype(BF16)
    own[...] = pts0
    w0 = dot(w[...], basis[...]).astype(BF16)
    low = pl.multiple_of(side * skeleton, skeleton)
    pts1 = dot(pts0, one_hot(upper[0, 0:1], skeleton, low)).astype(BF16)
    w1 = dot(w0, ubasis[0, 0, pl.ds(low, skeleton), :]).astype(BF16)
    low = pl.multiple_of(child * skeleton, skeleton)
    pts2 = dot(pts1, one_hot(upper[0, 1:2], skeleton, low))
    w2 = dot(w1, ubasis[0, 1, pl.ds(low, skeleton), :]).astype(BF16)
    quarter = skeleton // GROUP
    share = sum(pts2[:, at * quarter : (at + 1) * quarter] for at in range(GROUP))
    packed = feats // GROUP
    share = jnp.concatenate(
        [share[at * packed : (at + 1) * packed] for at in range(GROUP)], axis=1
    ).astype(BF16)
    for level, (weights, points) in enumerate(((w0, pts0), (w1, pts1), (w2, pts2.astype(BF16)))):
        block[level, 0:rhs] = weights
        block[level, rhs : rhs + feats] = points
        block[level, rhs + feats :] = share

    def send(to, carry):
        near = jnp.abs(to // 2 - me // 2) == 1
        away = jnp.abs(to // GROUP - me // GROUP) >= 2
        out[to] = block[jnp.where(near, 0, jnp.where(away, 2, 1))]
        return carry

    lax.fori_loop(0, out.shape[0], send, 0)


def listed_pairs(near, count, first, leaves, wanted, one, other):
    total = jnp.int32(0)
    for leaf in range(leaves):

        def note(slot, at, leaf=leaf):
            b = near[leaf, slot] - first
            keep, place = wanted(leaf, b)
            one[at] = leaf
            other[at] = place
            return at + keep.astype(jnp.int32)

        total = lax.fori_loop(0, count[leaf], note, total)
    for at in range(UNROLL - 1):
        one[total + at] = leaves
        other[total + at] = 0
    return (total + UNROLL - 1) // UNROLL


def inside_kernel(near, count, pts, w, out, source, target, weights, acc, one, other):
    feats, rows = pts.shape
    leaves = rows // LEAF
    spread = 0.5 * feats
    first = lax.axis_index("leaf") * leaves
    acc[...] = jnp.zeros_like(acc)
    target[leaves] = jnp.zeros_like(target[leaves])
    weights[leaves] = jnp.zeros_like(weights[leaves])
    for leaf in range(leaves):
        at = slice(leaf * LEAF, (leaf + 1) * LEAF)
        source[leaf] = padded(source_side(pts[:, at], spread), source.shape[2]).T
        target[leaf] = padded(target_side(pts[:, at], spread), target.shape[1])
        weights[leaf] = w[:, at]
    rounds = listed_pairs(
        near, count, first, leaves, lambda a, b: ((b > a) & (b < leaves), b), one, other
    )

    def tile(a, b):
        return jnp.exp(dot(source[b], target[a])).astype(BF16)

    def own(step, carry):
        tiles = [tile(step * UNROLL + at, step * UNROLL + at) for at in range(UNROLL)]
        for at in range(UNROLL):
            acc[step * UNROLL + at] += dot(weights[step * UNROLL + at], tiles[at])
        return carry

    lax.fori_loop(0, leaves // UNROLL, own, 0)

    def pair(step, carry):
        pairs = [(one[step * UNROLL + at], other[step * UNROLL + at]) for at in range(UNROLL)]
        tiles = [tile(a, b) for a, b in pairs]
        for (a, b), t in zip(pairs, tiles):
            acc[a] += dot(weights[b], t)
            acc[b] += dot_nt(weights[a], t)
        return carry

    lax.fori_loop(0, rounds, pair, 0)
    for leaf in range(leaves):
        out[:, leaf * LEAF : (leaf + 1) * LEAF] = acc[leaf]


def outside_kernel(near, count, pts, low, high, inside, out, source, target, weights, acc, one, other):
    feats, rows = pts.shape
    leaves = rows // LEAF
    reach = leaves - 1
    spread = 0.5 * feats
    first = lax.axis_index("leaf") * leaves
    target[leaves] = jnp.zeros_like(target[leaves])
    acc[leaves] = jnp.zeros_like(acc[leaves])
    for leaf in range(leaves):
        at = slice(leaf * LEAF, (leaf + 1) * LEAF)
        target[leaf] = padded(target_side(pts[:, at], spread), target.shape[1])
        acc[leaf] = inside[:, at]
    for ref, start, begin in ((low, 1, 0), (high, 0, reach)):
        for leaf in range(reach):
            at = slice((start + leaf) * LEAF, (start + leaf + 1) * LEAF)
            source[begin + leaf] = padded(source_side(ref[:feats, at], spread), source.shape[2]).T
            weights[begin + leaf] = ref[feats:, at]
    rounds = listed_pairs(
        near, count, first, leaves,
        lambda a, b: ((b < 0) | (b >= leaves), jnp.where(b < 0, b + reach, jnp.maximum(b - 1, 0))),
        one, other,
    )

    def pair(step, carry):
        pairs = [(one[step * UNROLL + at], other[step * UNROLL + at]) for at in range(UNROLL)]
        tiles = [jnp.exp(dot(source[b], target[a])).astype(BF16) for a, b in pairs]
        for (a, b), t in zip(pairs, tiles):
            acc[a] += dot(weights[b], t)
        return carry

    lax.fori_loop(0, rounds, pair, 0)
    for leaf in range(leaves):
        out[:, leaf * LEAF : (leaf + 1) * LEAF] = acc[leaf]


def downward_kernel(far, got, own, ubasis, basis, near, out, top):
    me = lax.axis_index("leaf")
    side = lax.rem(me, 2)
    child = lax.rem(me // 2, 2)
    feats, skeleton = own.shape
    rhs = near.shape[0]
    spread = 0.5 * feats
    slots = far.shape[1] // 2
    quarter = skeleton // GROUP
    packed = feats // GROUP

    def node(start, span):
        parts = got[start].astype(F32)
        for at in range(1, span):
            parts = parts + got[start + at].astype(F32)
        parts = parts.astype(BF16)
        return parts[0:rhs], parts[rhs : rhs + feats]

    def potential(aim, weights, points):
        tile = jnp.exp(dot_tn(source_side(points, spread), aim)).astype(BF16)
        return dot(weights, tile)

    def listed(level, aim):
        total = jnp.zeros((rhs, skeleton), F32)
        for slot in range(slots):
            k = far[0, level * slots + slot]
            weights, points = node(jnp.maximum(k, 0) * 2**level, 2**level)
            total = total + jnp.where(k >= 0, potential(aim, weights, points), 0.0)
        return total

    v0 = listed(0, target_side(own[...], spread))
    v1 = listed(1, target_side(node(me // 2 * 2, 2)[1], spread))
    shares = []
    for at in range(GROUP):
        share = got[me // GROUP * GROUP + at, rhs + feats :]
        shares.append(
            jnp.concatenate(
                [share[:, part * quarter : (part + 1) * quarter] for part in range(GROUP)], axis=0
            )
        )
    aim = target_side(jnp.concatenate(shares, axis=1), spread)
    top[...] = jnp.zeros_like(top)

    def one_top(k, carry):
        @pl.when(jnp.abs(k - me // GROUP) >= 2)
        def _():
            weights, points = node(k * GROUP, GROUP)
            top[...] += potential(aim, weights, points)

        return carry

    lax.fori_loop(0, got.shape[0] // GROUP, one_top, 0)
    low = pl.multiple_of(child * skeleton, skeleton)
    z1 = v1 + dot_nt(top[...].astype(BF16), ubasis[0, 1, pl.ds(low, skeleton), :])
    low = pl.multiple_of(side * skeleton, skeleton)
    z0 = v0 + dot_nt(z1.astype(BF16), ubasis[0, 0, pl.ds(low, skeleton), :])
    out[...] = near[...] + dot_nt(z0.astype(BF16), basis[...])


def call(kernel, name, out, specs, scratch, flops):
    return pl.pallas_call(
        kernel,
        out_shape=out,
        in_specs=specs,
        out_specs=jax.tree.map(lambda _: VMEM, out),
        scratch_shapes=scratch,
        compiler_params=pltpu.CompilerParams(vmem_limit_bytes=LIMIT),
        cost_estimate=pl.CostEstimate(flops=flops, bytes_accessed=1 << 20, transcendentals=0),
        name=name,
    )


def per_device(
    points, charges, near_list, near_count, skel_index, basis, upper_index, upper_basis, far_list
):
    devices = lax.axis_size("leaf")
    rows, feats = points.shape
    rhs = charges.shape[1]
    skeleton = skel_index.shape[1]
    leaves = rows // LEAF
    depth = 128
    pts = points.T
    w = charges.T
    packed = jnp.concatenate([pts, w], axis=0)
    onward = [(i, i + 1) for i in range(devices - 1)]
    low = lax.ppermute(packed, "leaf", onward)
    high = lax.ppermute(packed, "leaf", [(b, a) for a, b in onward])
    height = rhs + feats + feats // GROUP
    sent, own = call(
        upward_kernel,
        "upward",
        (
            jax.ShapeDtypeStruct((devices, height, skeleton), BF16),
            jax.ShapeDtypeStruct((feats, skeleton), BF16),
        ),
        [VMEM] * 6,
        [pltpu.VMEM((3, height, skeleton), BF16)],
        int(1e9),
    )(pts, w, basis, skel_index, upper_index[0][None], upper_basis)
    got = lax.all_to_all(sent, "leaf", 0, 0)
    pairs = leaves * near_list.shape[1] + UNROLL
    lists = [pltpu.SMEM((pairs,), jnp.int32)] * 2
    field = jax.ShapeDtypeStruct((rhs, rows), F32)
    near = call(
        inside_kernel,
        "near_inside",
        field,
        [SMEM, SMEM, VMEM, VMEM],
        [
            pltpu.VMEM((leaves, LEAF, depth), BF16),
            pltpu.VMEM((leaves + 1, depth, LEAF), BF16),
            pltpu.VMEM((leaves + 1, rhs, LEAF), BF16),
            pltpu.VMEM((leaves + 1, rhs, LEAF), F32),
            *lists,
        ],
        int(8e9),
    )(near_list, near_count, pts, w)
    reach = leaves - 1
    near = call(
        outside_kernel,
        "near_outside",
        field,
        [SMEM, SMEM, VMEM, VMEM, VMEM, VMEM],
        [
            pltpu.VMEM((2 * reach, LEAF, depth), BF16),
            pltpu.VMEM((leaves + 1, depth, LEAF), BF16),
            pltpu.VMEM((2 * reach, rhs, LEAF), BF16),
            pltpu.VMEM((leaves + 1, rhs, LEAF), F32),
            *lists,
        ],
        int(8e9),
    )(near_list, near_count, pts, low, high, near)
    field = call(
        downward_kernel,
        "downward",
        field,
        [SMEM, VMEM, VMEM, VMEM, VMEM, VMEM],
        [pltpu.VMEM((rhs, skeleton), F32)],
        int(1e9),
    )(far_list.reshape(1, -1), got, own, upper_basis, basis, near)
    return field.T


def solution(mesh):
    both = ("clips", "leaf")
    in_specs = (
        P(both, None),
        P(both, None),
        P(both, None),
        P(both),
        P(both, None),
        P(both, None),
        P(both, None, None),
        P(both, None, None, None),
        P(both, None, None),
    )
    return jax.shard_map(
        per_device, mesh=mesh, in_specs=in_specs, out_specs=P(both, None), check_vma=False
    )
```

```python
import jax
import jax.numpy as jnp
from jax import lax
from jax.experimental import pallas as pl
from jax.experimental.pallas import tpu as pltpu
from jax.sharding import PartitionSpec as P

LEAF = 512
GROUP = 4
UNROLL = 4
CODE = 32
TOPS = 4
EXTRA = 16
VMEM = pl.BlockSpec(memory_space=pltpu.VMEM)
SMEM = pl.BlockSpec(memory_space=pltpu.SMEM)
LIMIT = 28 << 20
F32 = jnp.float32
BF16 = jnp.bfloat16


def dot(left, right):
    return jnp.dot(left, right, preferred_element_type=F32)


def dot_nt(left, right):
    return lax.dot_general(left, right, (((1,), (1,)), ((), ())), preferred_element_type=F32)


def dot_tn(left, right):
    return lax.dot_general(left, right, (((0,), (0,)), ((), ())), preferred_element_type=F32)


def norm_rows(feats, spread, ones_first):
    norm = jnp.sum(feats * feats, axis=0, keepdims=True) * (-1.0 / spread)
    high = norm.astype(BF16).astype(F32)
    mid = (norm - high).astype(BF16).astype(F32)
    low = norm - high - mid
    row = lax.broadcasted_iota(jnp.int32, (EXTRA, feats.shape[1]), 0)
    start = 3 if ones_first else 0
    rows = jnp.where((row >= 3 - start) & (row < 6 - start), 1.0, 0.0)
    for at, piece in enumerate((high, mid, low)):
        rows = jnp.where(row == start + at, piece, rows)
    return rows.astype(BF16)


def source_side(feats, spread):
    return jnp.concatenate([feats, norm_rows(feats.astype(F32), spread, False)], axis=0)


def target_side(feats, spread):
    feats_f = feats.astype(F32)
    scaled = (feats_f * (2.0 / spread)).astype(BF16)
    return jnp.concatenate([scaled, norm_rows(feats_f, spread, True)], axis=0)


def padded(rows, height):
    gap = height - rows.shape[0]
    return jnp.concatenate([rows, jnp.zeros((gap, rows.shape[1]), rows.dtype)], axis=0)


def one_hot(index, height, offset):
    rows = lax.broadcasted_iota(jnp.int32, (height, index.shape[1]), 0) + offset
    return jnp.where(rows == index, 1.0, 0.0).astype(BF16)


def upward_kernel(pts, w, basis, skel, upper, ubasis, out, own, block):
    me = lax.axis_index("leaf")
    side = lax.rem(me, 2)
    child = lax.rem(me // 2, 2)
    feats, rows = pts.shape
    rhs = w.shape[0]
    skeleton = basis.shape[1]
    half = rows // 2
    lanes = skeleton // 2
    picks = [
        dot(
            pts[:, at * half : (at + 1) * half],
            one_hot(skel[:, at * lanes : (at + 1) * lanes], half, at * half),
        )
        for at in range(2)
    ]
    pts0 = jnp.concatenate(picks, axis=1).astype(BF16)
    own[...] = pts0
    low = pl.multiple_of(side * skeleton, skeleton)
    pts1 = dot(pts0, one_hot(upper[0, 0:1], skeleton, low)).astype(BF16)
    up = pl.multiple_of(child * skeleton, skeleton)
    pts2 = dot(pts1, one_hot(upper[0, 1:2], skeleton, up))
    quarter = skeleton // GROUP
    share = sum(pts2[:, at * quarter : (at + 1) * quarter] for at in range(GROUP))
    packed = feats // GROUP
    share = jnp.concatenate(
        [share[at * packed : (at + 1) * packed] for at in range(GROUP)], axis=1
    ).astype(BF16)
    for level, points in enumerate((pts0, pts1, pts2.astype(BF16))):
        block[level, rhs : rhs + feats] = points
        block[level, rhs + feats :] = share
    w0 = dot(w[...], basis[...]).astype(BF16)
    w1 = dot(w0, ubasis[0, 0, pl.ds(low, skeleton), :]).astype(BF16)
    w2 = dot(w1, ubasis[0, 1, pl.ds(up, skeleton), :]).astype(BF16)
    for level, weights in enumerate((w0, w1, w2)):
        block[level, 0:rhs] = weights

    def send(to, carry):
        near = jnp.abs(to // 2 - me // 2) == 1
        away = jnp.abs(to // GROUP - me // GROUP) >= 2
        out[to] = block[jnp.where(near, 0, jnp.where(away, 2, 1))]
        return carry

    lax.fori_loop(0, out.shape[0], send, 0)


def note_pairs(near, count, first, leaves, lists):
    ends = tuple(jnp.int32(0) for _ in lists)
    for leaf in range(leaves):

        def note(slot, ends, leaf=leaf):
            b = near[leaf, slot] - first
            after = []
            for end, (to, wanted) in zip(ends, lists):
                keep, place = wanted(leaf, b)
                to[end] = place + leaf * CODE
                after.append(end + keep.astype(jnp.int32))
            return tuple(after)

        ends = lax.fori_loop(0, count[leaf], note, ends)
    for end, (to, _) in zip(ends, lists):
        for at in range(UNROLL):
            to[end + at] = leaves * CODE
    return ends


def over_pairs(todo, length, work):
    def decoded(start, span):
        codes = [todo[start + at] for at in range(span)]
        return [(code // CODE, lax.rem(code, CODE)) for code in codes]

    def step(at, carry):
        work(decoded(at * UNROLL, UNROLL))
        return carry

    rounds = (length + 1) // UNROLL
    lax.fori_loop(0, rounds, step, 0)

    @pl.when(rounds * UNROLL < length)
    def _():
        work(decoded(rounds * UNROLL, 2))


def halo_place(b, leaves):
    return jnp.where(b < 0, b + leaves, jnp.maximum(b - leaves, 0))


def inside_kernel(
    near, count, pts, w, mate_in, out, mate, target, source, weights, acc, pairs, singles, sem
):
    feats, rows = pts.shape
    leaves = rows // LEAF
    spread = 0.5 * feats
    load = pltpu.make_async_copy(mate_in, mate, sem)
    load.start()
    me = lax.axis_index("leaf")
    even = lax.rem(me, 2) == 0
    lengths = note_pairs(
        near, count, me * leaves, leaves,
        (
            (pairs, lambda a, b: ((b > a) & (b < leaves), jnp.clip(b, 0, leaves - 1))),
            (
                singles,
                lambda a, b: (
                    ((b < 0) != even) & ((b < 0) | (b >= leaves)),
                    halo_place(b, leaves) + leaves,
                ),
            ),
        ),
    )
    acc[...] = jnp.zeros_like(acc)
    target[leaves] = jnp.zeros_like(target[leaves])
    for leaf in range(leaves):
        at = slice(leaf * LEAF, (leaf + 1) * LEAF)
        source[leaf] = padded(source_side(pts[:, at], spread), source.shape[2]).T
        target[leaf] = padded(target_side(pts[:, at], spread), target.shape[1])
        weights[leaf] = w[:, at]

    def tile(a, b):
        return jnp.exp(dot(source[b], target[a])).astype(BF16)

    def single(these):
        tiles = [tile(a, b) for a, b in these]
        for (a, b), t in zip(these, tiles):
            acc[a] += dot(weights[b], t)

    def pair(these):
        tiles = [tile(a, b) for a, b in these]
        for (a, b), t in zip(these, tiles):
            acc[a] += dot(weights[b], t)
            acc[b] += dot_nt(weights[a], t)

    def own(step, carry):
        single([(step * UNROLL + at, step * UNROLL + at) for at in range(UNROLL)])
        return carry

    weights[leaves] = jnp.zeros_like(weights[0])
    lax.fori_loop(0, leaves // UNROLL, own, 0)
    over_pairs(pairs, lengths[0], pair)
    load.wait()
    for leaf in range(leaves):
        at = slice(leaf * LEAF, (leaf + 1) * LEAF)
        source[leaves + leaf] = padded(source_side(mate[:feats, at], spread), source.shape[2]).T
        weights[leaves + leaf] = mate[feats:, at]
    over_pairs(singles, lengths[1], single)
    for leaf in range(leaves):
        out[:, leaf * LEAF : (leaf + 1) * LEAF] = acc[leaf]


def outside_kernel(
    near, count, pts, other_in, inside_in, out,
    other, inside, target, source, weights, acc, singles, sems,
):
    rhs, rows = inside.shape
    feats = pts.shape[0]
    leaves = rows // LEAF
    spread = 0.5 * feats
    moves = ((other_in, other), (inside_in, inside))
    loads = [pltpu.make_async_copy(a, b, sems.at[at]) for at, (a, b) in enumerate(moves)]
    for load in loads:
        load.start()
    me = lax.axis_index("leaf")
    even = lax.rem(me, 2) == 0
    lengths = note_pairs(
        near, count, me * leaves, leaves,
        (
            (
                singles,
                lambda a, b: (
                    ((b < 0) == even) & ((b < 0) | (b >= leaves)),
                    halo_place(b, leaves),
                ),
            ),
        ),
    )
    acc[leaves] = jnp.zeros_like(acc[leaves])
    target[leaves] = jnp.zeros_like(target[leaves])
    for load in loads:
        load.wait()
    for leaf in range(leaves):
        at = slice(leaf * LEAF, (leaf + 1) * LEAF)
        target[leaf] = padded(target_side(pts[:, at], spread), target.shape[1])
        acc[leaf] = inside[:, at]
    for leaf in range(leaves):
        at = slice(leaf * LEAF, (leaf + 1) * LEAF)
        source[leaf] = padded(source_side(other[:feats, at], spread), source.shape[2]).T
        weights[leaf] = other[feats:, at]

    def single(these):
        tiles = [jnp.exp(dot(source[b], target[a])).astype(BF16) for a, b in these]
        for (a, b), t in zip(these, tiles):
            acc[a] += dot(weights[b], t)

    over_pairs(singles, lengths[0], single)
    for leaf in range(leaves):
        out[:, leaf * LEAF : (leaf + 1) * LEAF] = acc[leaf]


def downward_kernel(far, got, own, ubasis, basis, near, out):
    me = lax.axis_index("leaf")
    side = lax.rem(me, 2)
    child = lax.rem(me // 2, 2)
    feats, skeleton = own.shape
    rhs = near.shape[0]
    spread = 0.5 * feats
    slots = far.shape[2]
    quarter = skeleton // GROUP

    def node(start, span):
        parts = got[start].astype(F32)
        for at in range(1, span):
            parts = parts + got[start + at].astype(F32)
        return parts[0:rhs], parts[rhs : rhs + feats].astype(BF16)

    def potential(aim, nodes):
        weights = [jnp.where(counts, w, 0.0).astype(BF16) for counts, w, _ in nodes]
        points = jnp.concatenate([p for _, _, p in nodes], axis=1)
        tile = jnp.exp(dot_tn(aim, source_side(points, spread))).astype(BF16)
        return dot_nt(jnp.concatenate(weights, axis=1), tile)

    def listed(level, aim):
        nodes = []
        for slot in range(slots):
            k = far[0, level, slot]
            nodes.append((k >= 0, *node(jnp.maximum(k, 0) * 2**level, 2**level)))
        return potential(aim, nodes)

    v0 = listed(0, target_side(own[...], spread))
    v1 = listed(1, target_side(node(me // 2 * 2, 2)[1], spread))
    shares = []
    for at in range(GROUP):
        share = got[me // GROUP * GROUP + at, rhs + feats :]
        shares.append(
            jnp.concatenate(
                [share[:, part * quarter : (part + 1) * quarter] for part in range(GROUP)], axis=0
            )
        )
    aim = target_side(jnp.concatenate(shares, axis=1), spread)
    tops = got.shape[0] // GROUP
    batch = min(tops, TOPS)

    def some_tops(step, total):
        nodes = []
        for at in range(batch):
            k = step * batch + at
            nodes.append((jnp.abs(k - me // GROUP) >= 2, *node(k * GROUP, GROUP)))
        return total + potential(aim, nodes)

    v2 = jnp.zeros((rhs, skeleton), F32)
    if tops == batch:
        v2 = some_tops(0, v2)
    else:
        v2 = lax.fori_loop(0, tops // batch, some_tops, v2)
    low = pl.multiple_of(child * skeleton, skeleton)
    z1 = v1 + dot_nt(v2.astype(BF16), ubasis[0, 1, pl.ds(low, skeleton), :])
    low = pl.multiple_of(side * skeleton, skeleton)
    z0 = v0 + dot_nt(z1.astype(BF16), ubasis[0, 0, pl.ds(low, skeleton), :])
    out[...] = near[...] + dot_nt(z0.astype(BF16), basis[...])


def call(kernel, name, out, specs, scratch, flops, alias={}):
    return pl.pallas_call(
        kernel,
        out_shape=out,
        in_specs=specs,
        out_specs=jax.tree.map(lambda _: VMEM, out),
        scratch_shapes=scratch,
        compiler_params=pltpu.CompilerParams(vmem_limit_bytes=LIMIT),
        cost_estimate=pl.CostEstimate(flops=flops, bytes_accessed=1 << 20, transcendentals=0),
        input_output_aliases=alias,
        name=name,
    )


def per_device(
    points, charges, near_list, near_count, skel_index, basis, upper_index, upper_basis, far_list
):
    devices = lax.axis_size("leaf")
    rows, feats = points.shape
    rhs = charges.shape[1]
    skeleton = skel_index.shape[1]
    leaves = rows // LEAF
    depth = 128
    pts = points.T
    w = charges.T
    halo = jnp.concatenate([pts, w], axis=0)
    mate = lax.ppermute(halo, "leaf", [(i, i ^ 1) for i in range(devices)])
    bridge = [(i, i + 1) for i in range(1, devices - 1, 2)]
    other_side = lax.ppermute(halo, "leaf", bridge + [(b, a) for a, b in bridge])
    height = rhs + feats + feats // GROUP
    sent, own = call(
        upward_kernel,
        "upward",
        (
            jax.ShapeDtypeStruct((devices, height, skeleton), BF16),
            jax.ShapeDtypeStruct((feats, skeleton), BF16),
        ),
        [VMEM] * 6,
        [pltpu.VMEM((3, height, skeleton), BF16)],
        int(1e9),
    )(pts, w, basis, skel_index, upper_index[0][None], upper_basis)
    got = lax.all_to_all(sent, "leaf", 0, 0)
    todo = pltpu.SMEM((leaves * near_list.shape[1] + UNROLL + 1,), jnp.int32)
    whole = pl.BlockSpec(memory_space=pl.ANY)
    field = jax.ShapeDtypeStruct((rhs, rows), F32)
    near = call(
        inside_kernel,
        "near_inside",
        field,
        [SMEM, SMEM, VMEM, VMEM, whole],
        [
            pltpu.VMEM(halo.shape, BF16),
            pltpu.VMEM((leaves + 1, depth, LEAF), BF16),
            pltpu.VMEM((2 * leaves, LEAF, depth), BF16),
            pltpu.VMEM((2 * leaves, rhs, LEAF), BF16),
            pltpu.VMEM((leaves + 1, rhs, LEAF), F32),
            todo,
            todo,
            pltpu.SemaphoreType.DMA,
        ],
        int(8e9),
    )(near_list, near_count, pts, w, mate)
    near = call(
        outside_kernel,
        "near_outside",
        field,
        [SMEM, SMEM, VMEM, whole, whole],
        [
            pltpu.VMEM(halo.shape, BF16),
            pltpu.VMEM((rhs, rows), F32),
            pltpu.VMEM((leaves + 1, depth, LEAF), BF16),
            pltpu.VMEM((leaves, LEAF, depth), BF16),
            pltpu.VMEM((leaves, rhs, LEAF), BF16),
            pltpu.VMEM((leaves + 1, rhs, LEAF), F32),
            todo,
            pltpu.SemaphoreType.DMA((2,)),
        ],
        int(8e9),
    )(near_list, near_count, pts, other_side, near)
    field = call(
        downward_kernel,
        "downward",
        field,
        [SMEM, VMEM, VMEM, VMEM, VMEM, VMEM],
        [],
        int(1e9),
        {5: 0},
    )(far_list, got, own, upper_basis, basis, near)
    return field.T


def solution(mesh):
    both = ("clips", "leaf")
    in_specs = (
        P(both, None),
        P(both, None),
        P(both, None),
        P(both),
        P(both, None),
        P(both, None),
        P(both, None, None),
        P(both, None, None, None),
        P(both, None, None),
    )
    return jax.shard_map(
        per_device, mesh=mesh, in_specs=in_specs, out_specs=P(both, None), check_vma=False
    )
```

```python
import jax
import jax.numpy as jnp
from jax import lax
from jax.experimental import pallas as pl
from jax.experimental.pallas import tpu as pltpu
from jax.sharding import PartitionSpec as P

LEAF = 512
GROUP = 4
UNROLL = 4
CUTS = 4
CODE = 32
TOPS = 2
EXTRA = 16
VMEM = pl.BlockSpec(memory_space=pltpu.VMEM)
SMEM = pl.BlockSpec(memory_space=pltpu.SMEM)
LIMIT = 28 << 20
F32 = jnp.float32
BF16 = jnp.bfloat16


def dot(left, right):
    return jnp.dot(left, right, preferred_element_type=F32)


def dot_nt(left, right):
    return lax.dot_general(left, right, (((1,), (1,)), ((), ())), preferred_element_type=F32)


def dot_tn(left, right):
    return lax.dot_general(left, right, (((0,), (0,)), ((), ())), preferred_element_type=F32)


def norm_rows(feats, spread, ones_first):
    norm = jnp.sum(feats * feats, axis=0, keepdims=True) * (-1.0 / spread)
    high = norm.astype(BF16).astype(F32)
    mid = (norm - high).astype(BF16).astype(F32)
    low = norm - high - mid
    row = lax.broadcasted_iota(jnp.int32, (EXTRA, feats.shape[1]), 0)
    start = 3 if ones_first else 0
    rows = jnp.where((row >= 3 - start) & (row < 6 - start), 1.0, 0.0)
    for at, piece in enumerate((high, mid, low)):
        rows = jnp.where(row == start + at, piece, rows)
    return rows.astype(BF16)


def source_side(feats, spread):
    return jnp.concatenate([feats, norm_rows(feats.astype(F32), spread, False)], axis=0)


def target_side(feats, spread):
    feats_f = feats.astype(F32)
    scaled = (feats_f * (2.0 / spread)).astype(BF16)
    return jnp.concatenate([scaled, norm_rows(feats_f, spread, True)], axis=0)


def padded(rows, height):
    gap = height - rows.shape[0]
    return jnp.concatenate([rows, jnp.zeros((gap, rows.shape[1]), rows.dtype)], axis=0)


def one_hot(index, height, offset):
    rows = lax.broadcasted_iota(jnp.int32, (height, index.shape[1]), 0) + offset
    return jnp.where(rows == index, 1.0, 0.0).astype(BF16)


def chosen_first(upper, side, skeleton):
    half = skeleton // 2
    kept = upper[0, 0:1, pl.ds(pl.multiple_of(side * half, half), half)] - side * skeleton
    pair = lax.broadcasted_iota(jnp.int32, kept.shape, 1)
    order = jnp.concatenate([kept, 4 * pair + 1 - kept], axis=1)
    return one_hot(order, skeleton, 0)


def points_kernel(pts, skel, upper, out, own):
    me = lax.axis_index("leaf")
    side = lax.rem(me, 2)
    child = lax.rem(me // 2, 2)
    rows = pts.shape[1]
    skeleton = own.shape[1]
    half = rows // 2
    lanes = skeleton // 2
    picks = [
        dot(
            pts[:, at * half : (at + 1) * half],
            one_hot(skel[:, at * lanes : (at + 1) * lanes], half, at * half),
        )
        for at in range(2)
    ]
    pts0 = jnp.concatenate(picks, axis=1).astype(BF16)
    own[...] = pts0
    out[0] = dot(pts0, chosen_first(upper, side, skeleton)).astype(BF16)
    pts1 = dot(pts0, one_hot(upper[0, 0:1], skeleton, side * skeleton)).astype(BF16)
    out[1] = pts1
    out[2] = dot(pts1, one_hot(upper[0, 1:2], skeleton, child * skeleton)).astype(BF16)


def weights_kernel(w, basis, upper, ubasis, points, out, block):
    me = lax.axis_index("leaf")
    side = lax.rem(me, 2)
    child = lax.rem(me // 2, 2)
    rhs = w.shape[0]
    skeleton = basis.shape[1]
    w0 = dot(w[...], basis[...]).astype(BF16)
    low = pl.multiple_of(side * skeleton, skeleton)
    w1 = dot(w0, ubasis[0, 0, pl.ds(low, skeleton), :]).astype(BF16)
    up = pl.multiple_of(child * skeleton, skeleton)
    w2 = dot(w1, ubasis[0, 1, pl.ds(up, skeleton), :]).astype(BF16)
    block[0, 0:rhs] = dot(w0, chosen_first(upper, side, skeleton)).astype(BF16)
    block[1, 0:rhs] = w1
    block[2, 0:rhs] = w2
    block[:, rhs:] = points[...]

    def send(to, carry):
        near = jnp.abs(to // 2 - me // 2) == 1
        away = jnp.abs(to // GROUP - me // GROUP) >= 2
        out[to] = block[jnp.where(near, 0, jnp.where(away, 2, 1))]
        return carry

    lax.fori_loop(0, out.shape[0], send, 0)


def note_pairs(near, count, first, leaves, lists, starts):
    ends = tuple(jnp.int32(start) for start in starts)
    for leaf in range(leaves):

        def note(slot, ends, leaf=leaf):
            b = near[leaf, slot] - first
            after = []
            for end, (to, wanted) in zip(ends, lists):
                keep, place = wanted(leaf, b)
                to[end] = place + leaf * CODE
                after.append(end + keep.astype(jnp.int32))
            return tuple(after)

        ends = lax.fori_loop(0, count[leaf], note, ends)
    for end, (to, _) in zip(ends, lists):
        for at in range(UNROLL):
            to[end + at] = leaves * CODE
    return ends


def over_pairs(todo, length, unroll, work):
    def decoded(start, span):
        codes = [todo[start + at] for at in range(span)]
        return [(code // CODE, lax.rem(code, CODE)) for code in codes]

    def step(at, carry):
        work(decoded(at * unroll, unroll))
        return carry

    rounds = (length + 1) // unroll
    lax.fori_loop(0, rounds, step, 0)
    done = rounds * unroll
    span = unroll // 2
    while span >= 2:
        fits = length - done > span - 2

        @pl.when(fits)
        def _(done=done, span=span):
            work(decoded(done, span))

        done = done + jnp.where(fits, span, 0)
        span //= 2


def halo_place(b, leaves, held):
    return jnp.where(b < 0, b + held, jnp.maximum(b - leaves, 0))


def inside_kernel(
    near, count, held_in, mate_in, out, held, mate, target, source, weights, acc, pairs, singles, sems
):
    rhs = weights.shape[1]
    feats, rows = held.shape[0] - rhs, held.shape[1]
    leaves = rows // LEAF
    spread = 0.5 * feats
    moves = ((held_in, held), (mate_in, mate))
    loads = [pltpu.make_async_copy(a, b, sems.at[at]) for at, (a, b) in enumerate(moves)]
    for load in loads:
        load.start()
    me = lax.axis_index("leaf")
    even = lax.rem(me, 2) == 0
    for leaf in range(leaves):
        singles[leaf] = leaf * CODE + leaf
    lengths = note_pairs(
        near, count, me * leaves, leaves,
        (
            (pairs, lambda a, b: ((b > a) & (b < leaves), jnp.clip(b, 0, leaves - 1))),
            (
                singles,
                lambda a, b: (
                    ((b < 0) != even) & ((b < 0) | (b >= leaves)),
                    halo_place(b, leaves, leaves) + leaves,
                ),
            ),
        ),
        (0, leaves),
    )
    acc[...] = jnp.zeros_like(acc)
    target[leaves] = jnp.zeros_like(target[leaves])
    loads[0].wait()
    for leaf in range(leaves):
        at = slice(leaf * LEAF, (leaf + 1) * LEAF)
        source[leaf] = padded(source_side(held[:feats, at], spread), source.shape[2]).T
        target[leaf] = padded(target_side(held[:feats, at], spread), target.shape[1])
        weights[leaf] = held[feats:, at]

    def tile(a, b):
        return jnp.exp(dot(source[b], target[a])).astype(BF16)

    def single(these):
        tiles = [tile(a, b) for a, b in these]
        for (a, b), t in zip(these, tiles):
            acc[a] += dot(weights[b], t)

    def pair(these):
        tiles = [tile(a, b) for a, b in these]
        for (a, b), t in zip(these, tiles):
            acc[a] += dot(weights[b], t)
            acc[b] += dot_nt(weights[a], t)

    weights[leaves] = jnp.zeros_like(weights[0])
    over_pairs(pairs, lengths[0], 2 * UNROLL, pair)
    loads[1].wait()
    for leaf in range(leaves):
        at = slice(leaf * LEAF, (leaf + 1) * LEAF)
        source[leaves + leaf] = padded(source_side(mate[:feats, at], spread), source.shape[2]).T
        weights[leaves + leaf] = mate[feats:, at]
    over_pairs(singles, lengths[1], 2 * UNROLL, single)
    for leaf in range(leaves):
        out[:, leaf * LEAF : (leaf + 1) * LEAF] = acc[leaf]


def outside_kernel(
    near, count, held_in, other_in, inside_in, out,
    held, other, inside, target, source, weights, acc, singles, sems,
):
    rhs, rows = inside.shape
    feats = held.shape[0] - rhs
    leaves = rows // LEAF
    spread = 0.5 * feats
    moves = ((held_in, held), (other_in, other), (inside_in, inside))
    loads = [pltpu.make_async_copy(a, b, sems.at[at]) for at, (a, b) in enumerate(moves)]
    for load in loads:
        load.start()
    me = lax.axis_index("leaf")
    even = lax.rem(me, 2) == 0
    lengths = note_pairs(
        near, count, me * leaves, leaves,
        (
            (
                singles,
                lambda a, b: (
                    ((b < 0) == even) & ((b < 0) | (b >= leaves)),
                    halo_place(b, leaves, leaves),
                ),
            ),
        ),
        (0,),
    )
    acc[leaves] = jnp.zeros_like(acc[leaves])
    target[leaves] = jnp.zeros_like(target[leaves])
    for load in loads:
        load.wait()
    for leaf in range(leaves):
        at = slice(leaf * LEAF, (leaf + 1) * LEAF)
        target[leaf] = padded(target_side(held[:feats, at], spread), target.shape[1])
        acc[leaf] = inside[:, at]
    for leaf in range(leaves):
        at = slice(leaf * LEAF, (leaf + 1) * LEAF)
        source[leaf] = padded(source_side(other[:feats, at], spread), source.shape[2]).T
        weights[leaf] = other[feats:, at]

    def single(these):
        tiles = [jnp.exp(dot(source[b], target[a])).astype(BF16) for a, b in these]
        for (a, b), t in zip(these, tiles):
            acc[a] += dot(weights[b], t)

    over_pairs(singles, lengths[0], 2 * UNROLL, single)
    for leaf in range(leaves):
        out[:, leaf * LEAF : (leaf + 1) * LEAF] = acc[leaf]


def downward_kernel(
    far, got, own, upper, ubasis_in, basis_in, near_in, out,
    ubasis, basis, near, done, in_sems, out_sems,
):
    me = lax.axis_index("leaf")
    side = lax.rem(me, 2)
    child = lax.rem(me // 2, 2)
    feats, skeleton = own.shape
    rhs = near.shape[0]
    halves = [pl.ds(pl.multiple_of(at * skeleton, skeleton), skeleton) for at in (side, child)]
    moves = [
        (ubasis_in.at[0, 1, halves[1]], ubasis.at[1]),
        (ubasis_in.at[0, 0, halves[0]], ubasis.at[0]),
        (near_in, near),
        (basis_in, basis),
    ]
    loads = [pltpu.make_async_copy(a, b, in_sems.at[at]) for at, (a, b) in enumerate(moves)]
    for load in loads:
        load.start()
    spread = 0.5 * feats
    slots = far.shape[2]

    def node(start, span):
        parts = got[start].astype(F32)
        for at in range(1, span):
            parts = parts + got[start + at].astype(F32)
        return parts[0:rhs], parts[rhs : rhs + feats].astype(BF16)

    def potential(aim, nodes):
        weights = [jnp.where(counts, w, 0.0).astype(BF16) for counts, w, _ in nodes]
        points = jnp.concatenate([p for _, _, p in nodes], axis=1)
        tile = jnp.exp(dot_tn(aim, source_side(points, spread))).astype(BF16)
        return dot_nt(jnp.concatenate(weights, axis=1), tile)

    def listed(level, aim):
        nodes = []
        for slot in range(slots):
            k = far[0, level, slot]
            nodes.append((k >= 0, *node(jnp.maximum(k, 0) * 2**level, 2**level)))
        return potential(aim, nodes)

    v0 = listed(0, target_side(own[...], spread))
    mine = node(me // 2 * 2, 2)[1]
    beside = me // GROUP * GROUP + 2 * (1 - child)
    half = skeleton // 2
    theirs = jnp.concatenate([got[beside + at, rhs:, :half] for at in range(2)], axis=1)
    lower = jnp.where(child == 0, mine, theirs)
    higher = jnp.where(child == 0, theirs, mine)
    joined = jnp.concatenate([lower, higher], axis=1)
    v1 = listed(1, target_side(mine, spread))
    aim = target_side(
        dot(joined, one_hot(upper[0, 1:2], 2 * skeleton, 0)).astype(BF16), spread
    )
    tops = got.shape[0] // GROUP
    top = me // GROUP
    gap = jnp.maximum(top - 1, 0)
    width = top + 2 - gap
    batch = min(tops - 2, TOPS)

    def some_tops(step, total):
        nodes = []
        for at in range(batch):
            place = step * batch + at
            k = place + jnp.where(place < gap, 0, width)
            nodes.append((k < tops, *node(jnp.minimum(k, tops - 1) * GROUP, GROUP)))
        return total + potential(aim, nodes)

    v2 = jnp.zeros((rhs, skeleton), F32)
    if tops - 2 == batch:
        v2 = some_tops(0, v2)
    else:
        v2 = lax.fori_loop(0, (tops - 2 + batch - 1) // batch, some_tops, v2)
    for load in loads:
        load.wait()
    z1 = v1 + dot_nt(v2.astype(BF16), ubasis[1])
    z0 = v0 + dot_nt(z1.astype(BF16), ubasis[0])
    z0 = z0.astype(BF16)
    part = near.shape[1] // CUTS
    copies = []
    for at in range(CUTS):
        cut = slice(at * part, (at + 1) * part)
        done[:, cut] = near[:, cut] + dot_nt(z0, basis[cut])
        lane = pl.ds(at * part, part)
        copy = pltpu.make_async_copy(done.at[:, lane], out.at[:, lane], out_sems.at[at])
        copy.start()
        copies.append(copy)
    for copy in copies:
        copy.wait()


def call(kernel, name, out, specs, scratch, flops, alias={}, outs=None, moved=1 << 20):
    return pl.pallas_call(
        kernel,
        out_shape=out,
        in_specs=specs,
        out_specs=jax.tree.map(lambda _: VMEM, out) if outs is None else outs,
        scratch_shapes=scratch,
        compiler_params=pltpu.CompilerParams(vmem_limit_bytes=LIMIT),
        cost_estimate=pl.CostEstimate(flops=flops, bytes_accessed=moved, transcendentals=0),
        input_output_aliases=alias,
        name=name,
    )


def per_device(
    points, charges, near_list, near_count, skel_index, basis, upper_index, upper_basis, far_list
):
    devices = lax.axis_size("leaf")
    rows, feats = points.shape
    rhs = charges.shape[1]
    skeleton = skel_index.shape[1]
    leaves = rows // LEAF
    depth = 128
    pts = points.T
    w = charges.T
    mates = [(i, i ^ 1) for i in range(devices)]
    bridge = [(i, i + 1) for i in range(1, devices - 1, 2)]
    bridge = bridge + [(b, a) for a, b in bridge]
    packed = jnp.concatenate([pts, w], axis=0)
    mate = lax.ppermute(packed, "leaf", mates)
    other = lax.ppermute(packed, "leaf", bridge)
    height = rhs + feats
    levels, own = call(
        points_kernel,
        "points",
        (
            jax.ShapeDtypeStruct((3, feats, skeleton), BF16),
            jax.ShapeDtypeStruct((feats, skeleton), BF16),
        ),
        [VMEM] * 3,
        [],
        int(1e9),
        moved=16 << 20,
    )(pts, skel_index, upper_index)
    sent = call(
        weights_kernel,
        "weights",
        jax.ShapeDtypeStruct((devices, height, skeleton), BF16),
        [VMEM] * 5,
        [pltpu.VMEM((3, height, skeleton), BF16)],
        int(1e9),
    )(w, basis, upper_index, upper_basis, levels)
    got = lax.all_to_all(sent, "leaf", 0, 0)
    todo = pltpu.SMEM((leaves * (near_list.shape[1] + 1) + UNROLL + 1,), jnp.int32)
    whole = pl.BlockSpec(memory_space=pl.ANY)
    field = jax.ShapeDtypeStruct((rhs, rows), F32)
    near = call(
        inside_kernel,
        "near_inside",
        field,
        [SMEM, SMEM, whole, whole],
        [
            pltpu.VMEM(packed.shape, BF16),
            pltpu.VMEM(packed.shape, BF16),
            pltpu.VMEM((leaves + 1, depth, LEAF), BF16),
            pltpu.VMEM((2 * leaves, LEAF, depth), BF16),
            pltpu.VMEM((2 * leaves, rhs, LEAF), BF16),
            pltpu.VMEM((leaves + 1, rhs, LEAF), F32),
            todo,
            todo,
            pltpu.SemaphoreType.DMA((2,)),
        ],
        int(8e9),
    )(near_list, near_count, packed, mate)
    near = call(
        outside_kernel,
        "near_outside",
        field,
        [SMEM, SMEM, whole, whole, whole],
        [
            pltpu.VMEM(packed.shape, BF16),
            pltpu.VMEM(packed.shape, BF16),
            pltpu.VMEM((rhs, rows), F32),
            pltpu.VMEM((leaves + 1, depth, LEAF), BF16),
            pltpu.VMEM((leaves, LEAF, depth), BF16),
            pltpu.VMEM((leaves, rhs, LEAF), BF16),
            pltpu.VMEM((leaves + 1, rhs, LEAF), F32),
            todo,
            pltpu.SemaphoreType.DMA((3,)),
        ],
        int(8e9),
    )(near_list, near_count, packed, other, near)
    field = call(
        downward_kernel,
        "downward",
        field,
        [SMEM, VMEM, VMEM, VMEM, whole, whole, whole],
        [
            pltpu.VMEM((2, skeleton, skeleton), BF16),
            pltpu.VMEM(basis.shape, BF16),
            pltpu.VMEM((rhs, rows), F32),
            pltpu.VMEM((rhs, rows), F32),
            pltpu.SemaphoreType.DMA((4,)),
            pltpu.SemaphoreType.DMA((CUTS,)),
        ],
        int(1e11),
        {6: 0},
        outs=whole,
        moved=0,
    )(far_list, got, own, upper_index, upper_basis, basis, near)
    return field.T


def solution(mesh):
    both = ("clips", "leaf")
    in_specs = (
        P(both, None),
        P(both, None),
        P(both, None),
        P(both),
        P(both, None),
        P(both, None),
        P(both, None, None),
        P(both, None, None, None),
        P(both, None, None),
    )
    return jax.shard_map(
        per_device, mesh=mesh, in_specs=in_specs, out_specs=P(both, None), check_vma=False
    )
```

```python
import jax
import jax.numpy as jnp
from jax import lax
from jax.experimental import pallas as pl
from jax.experimental.pallas import tpu as pltpu
from jax.sharding import PartitionSpec as P

LEAF = 512
GROUP = 4
UNROLL = 4
CUTS = 4
CODE = 32
TOPS = 2
EXTRA = 16
VMEM = pl.BlockSpec(memory_space=pltpu.VMEM)
SMEM = pl.BlockSpec(memory_space=pltpu.SMEM)
LIMIT = 28 << 20
F32 = jnp.float32
BF16 = jnp.bfloat16


def dot(left, right):
    return jnp.dot(left, right, preferred_element_type=F32)


def dot_nt(left, right):
    return lax.dot_general(left, right, (((1,), (1,)), ((), ())), preferred_element_type=F32)


def dot_tn(left, right):
    return lax.dot_general(left, right, (((0,), (0,)), ((), ())), preferred_element_type=F32)


def norm_rows(feats, spread, ones_first):
    norm = jnp.sum(feats * feats, axis=0, keepdims=True) * (-1.0 / spread)
    high = norm.astype(BF16).astype(F32)
    mid = (norm - high).astype(BF16).astype(F32)
    low = norm - high - mid
    row = lax.broadcasted_iota(jnp.int32, (EXTRA, feats.shape[1]), 0)
    start = 3 if ones_first else 0
    rows = jnp.where((row >= 3 - start) & (row < 6 - start), 1.0, 0.0)
    for at, piece in enumerate((high, mid, low)):
        rows = jnp.where(row == start + at, piece, rows)
    return rows.astype(BF16)


def source_side(feats, spread):
    return jnp.concatenate([feats, norm_rows(feats.astype(F32), spread, False)], axis=0)


def target_side(feats, spread):
    feats_f = feats.astype(F32)
    scaled = (feats_f * (2.0 / spread)).astype(BF16)
    return jnp.concatenate([scaled, norm_rows(feats_f, spread, True)], axis=0)


def padded(rows, height):
    gap = height - rows.shape[0]
    return jnp.concatenate([rows, jnp.zeros((gap, rows.shape[1]), rows.dtype)], axis=0)


def one_hot(index, height, offset):
    rows = lax.broadcasted_iota(jnp.int32, (height, index.shape[1]), 0) + offset
    return jnp.where(rows == index, 1.0, 0.0).astype(BF16)


def chosen_first(upper, side, skeleton):
    half = skeleton // 2
    kept = upper[0, 0:1, pl.ds(pl.multiple_of(side * half, half), half)] - side * skeleton
    pair = lax.broadcasted_iota(jnp.int32, kept.shape, 1)
    order = jnp.concatenate([kept, 4 * pair + 1 - kept], axis=1)
    return one_hot(order, skeleton, 0)


def points_kernel(pts, skel, upper, out, own):
    me = lax.axis_index("leaf")
    side = lax.rem(me, 2)
    child = lax.rem(me // 2, 2)
    rows = pts.shape[1]
    skeleton = own.shape[1]
    half = rows // 2
    lanes = skeleton // 2
    picks = [
        dot(
            pts[:, at * half : (at + 1) * half],
            one_hot(skel[:, at * lanes : (at + 1) * lanes], half, at * half),
        )
        for at in range(2)
    ]
    pts0 = jnp.concatenate(picks, axis=1).astype(BF16)
    own[...] = pts0
    out[0] = dot(pts0, chosen_first(upper, side, skeleton)).astype(BF16)
    pts1 = dot(pts0, one_hot(upper[0, 0:1], skeleton, side * skeleton)).astype(BF16)
    out[1] = pts1
    out[2] = dot(pts1, one_hot(upper[0, 1:2], skeleton, child * skeleton)).astype(BF16)


def weights_kernel(w, basis, upper, ubasis, points, out, block):
    me = lax.axis_index("leaf")
    side = lax.rem(me, 2)
    child = lax.rem(me // 2, 2)
    rhs = w.shape[0]
    skeleton = basis.shape[1]
    w0 = dot(w[...], basis[...]).astype(BF16)
    low = pl.multiple_of(side * skeleton, skeleton)
    w1 = dot(w0, ubasis[0, 0, pl.ds(low, skeleton), :]).astype(BF16)
    up = pl.multiple_of(child * skeleton, skeleton)
    w2 = dot(w1, ubasis[0, 1, pl.ds(up, skeleton), :]).astype(BF16)
    block[0, 0:rhs] = dot(w0, chosen_first(upper, side, skeleton)).astype(BF16)
    block[1, 0:rhs] = w1
    block[2, 0:rhs] = w2
    block[:, rhs:] = points[...]

    def send(to, carry):
        near = jnp.abs(to // 2 - me // 2) == 1
        away = jnp.abs(to // GROUP - me // GROUP) >= 2
        out[to] = block[jnp.where(near, 0, jnp.where(away, 2, 1))]
        return carry

    lax.fori_loop(0, out.shape[0], send, 0)


def note_pairs(near, count, first, leaves, lists, starts):
    ends = tuple(jnp.int32(start) for start in starts)
    for leaf in range(leaves):

        def note(slot, ends, leaf=leaf):
            b = near[leaf, slot] - first
            after = []
            for end, (to, wanted) in zip(ends, lists):
                keep, place = wanted(leaf, b)
                to[end] = place + leaf * CODE
                after.append(end + keep.astype(jnp.int32))
            return tuple(after)

        ends = lax.fori_loop(0, count[leaf], note, ends)
    for end, (to, _) in zip(ends, lists):
        for at in range(UNROLL):
            to[end + at] = leaves * CODE
    return ends


def over_pairs(todo, length, unroll, work):
    def decoded(start, span):
        codes = [todo[start + at] for at in range(span)]
        return [(code // CODE, lax.rem(code, CODE)) for code in codes]

    def step(at, carry):
        work(decoded(at * unroll, unroll))
        return carry

    rounds = (length + 1) // unroll
    lax.fori_loop(0, rounds, step, 0)
    done = rounds * unroll
    span = unroll // 2
    while span >= 2:
        fits = length - done > span - 2

        @pl.when(fits)
        def _(done=done, span=span):
            work(decoded(done, span))

        done = done + jnp.where(fits, span, 0)
        span //= 2


def halo_place(b, leaves, held):
    return jnp.where(b < 0, b + held, jnp.maximum(b - leaves, 0))


def inside_kernel(
    near, count, held_in, mate_in, out, held, mate, target, source, weights, acc, pairs, singles, sems
):
    rhs = weights.shape[1]
    feats, rows = held.shape[0] - rhs, held.shape[1]
    leaves = rows // LEAF
    spread = 0.5 * feats
    moves = ((held_in, held), (mate_in, mate))
    loads = [pltpu.make_async_copy(a, b, sems.at[at]) for at, (a, b) in enumerate(moves)]
    for load in loads:
        load.start()
    me = lax.axis_index("leaf")
    even = lax.rem(me, 2) == 0
    for leaf in range(leaves):
        singles[leaf] = leaf * CODE + leaf
    lengths = note_pairs(
        near, count, me * leaves, leaves,
        (
            (pairs, lambda a, b: ((b > a) & (b < leaves), jnp.clip(b, 0, leaves - 1))),
            (
                singles,
                lambda a, b: (
                    ((b < 0) != even) & ((b < 0) | (b >= leaves)),
                    halo_place(b, leaves, leaves) + leaves,
                ),
            ),
        ),
        (0, leaves),
    )
    acc[...] = jnp.zeros_like(acc)
    target[leaves] = jnp.zeros_like(target[leaves])
    loads[0].wait()
    for leaf in range(leaves):
        at = slice(leaf * LEAF, (leaf + 1) * LEAF)
        source[leaf] = padded(source_side(held[:feats, at], spread), source.shape[2]).T
        target[leaf] = padded(target_side(held[:feats, at], spread), target.shape[1])
        weights[leaf] = held[feats:, at]

    def tile(a, b):
        return jnp.exp(dot(source[b], target[a])).astype(BF16)

    def single(these):
        tiles = [tile(a, b) for a, b in these]
        for (a, b), t in zip(these, tiles):
            acc[a] += dot(weights[b], t)

    def pair(these):
        tiles = [tile(a, b) for a, b in these]
        for (a, b), t in zip(these, tiles):
            acc[a] += dot(weights[b], t)
            acc[b] += dot_nt(weights[a], t)

    weights[leaves] = jnp.zeros_like(weights[0])
    over_pairs(pairs, lengths[0], 2 * UNROLL, pair)
    loads[1].wait()
    for leaf in range(leaves):
        at = slice(leaf * LEAF, (leaf + 1) * LEAF)
        source[leaves + leaf] = padded(source_side(mate[:feats, at], spread), source.shape[2]).T
        weights[leaves + leaf] = mate[feats:, at]
    over_pairs(singles, lengths[1], 2 * UNROLL, single)
    for leaf in range(leaves):
        out[:, leaf * LEAF : (leaf + 1) * LEAF] = acc[leaf]


def outside_kernel(
    near, count, held, other_in, inside_in, out,
    other, inside, target, source, weights, acc, singles, sems,
):
    rhs, rows = inside.shape
    feats = held.shape[0] - rhs
    leaves = rows // LEAF
    spread = 0.5 * feats
    moves = ((inside_in, inside), (other_in, other))
    loads = [pltpu.make_async_copy(a, b, sems.at[at]) for at, (a, b) in enumerate(moves)]
    for load in loads:
        load.start()
    me = lax.axis_index("leaf")
    even = lax.rem(me, 2) == 0
    lengths = note_pairs(
        near, count, me * leaves, leaves,
        (
            (
                singles,
                lambda a, b: (
                    ((b < 0) == even) & ((b < 0) | (b >= leaves)),
                    halo_place(b, leaves, leaves),
                ),
            ),
        ),
        (0,),
    )
    acc[leaves] = jnp.zeros_like(acc[leaves])
    target[leaves] = jnp.zeros_like(target[leaves])
    loads[0].wait()
    for leaf in range(leaves):
        at = slice(leaf * LEAF, (leaf + 1) * LEAF)
        target[leaf] = padded(target_side(held[:feats, at], spread), target.shape[1])
        acc[leaf] = inside[:, at]
    loads[1].wait()
    for leaf in range(leaves):
        at = slice(leaf * LEAF, (leaf + 1) * LEAF)
        source[leaf] = padded(source_side(other[:feats, at], spread), source.shape[2]).T
        weights[leaf] = other[feats:, at]

    def single(these):
        tiles = [jnp.exp(dot(source[b], target[a])).astype(BF16) for a, b in these]
        for (a, b), t in zip(these, tiles):
            acc[a] += dot(weights[b], t)

    over_pairs(singles, lengths[0], 2 * UNROLL, single)
    for leaf in range(leaves):
        out[:, leaf * LEAF : (leaf + 1) * LEAF] = acc[leaf]


def downward_kernel(
    far, got, own, upper, ubasis_in, basis_in, near_in, out,
    ubasis, basis, near, done, in_sems, out_sems,
):
    me = lax.axis_index("leaf")
    side = lax.rem(me, 2)
    child = lax.rem(me // 2, 2)
    feats, skeleton = own.shape
    rhs = near.shape[0]
    halves = [pl.ds(pl.multiple_of(at * skeleton, skeleton), skeleton) for at in (side, child)]
    moves = [
        (ubasis_in.at[0, 1, halves[1]], ubasis.at[1]),
        (ubasis_in.at[0, 0, halves[0]], ubasis.at[0]),
        (near_in, near),
        (basis_in, basis),
    ]
    loads = [pltpu.make_async_copy(a, b, in_sems.at[at]) for at, (a, b) in enumerate(moves)]
    for load in loads:
        load.start()
    spread = 0.5 * feats
    slots = far.shape[2]

    def node(start, span):
        parts = got[start].astype(F32)
        for at in range(1, span):
            parts = parts + got[start + at].astype(F32)
        return parts[0:rhs], parts[rhs : rhs + feats].astype(BF16)

    def potential(aim, nodes):
        weights = [jnp.where(counts, w, 0.0).astype(BF16) for counts, w, _ in nodes]
        points = jnp.concatenate([p for _, _, p in nodes], axis=1)
        tile = jnp.exp(dot_tn(aim, source_side(points, spread))).astype(BF16)
        return dot_nt(jnp.concatenate(weights, axis=1), tile)

    def listed(level, aim):
        nodes = []
        for slot in range(slots):
            k = far[0, level, slot]
            nodes.append((k >= 0, *node(jnp.maximum(k, 0) * 2**level, 2**level)))
        return potential(aim, nodes)

    v0 = listed(0, target_side(own[...], spread))
    mine = node(me // 2 * 2, 2)[1]
    beside = me // GROUP * GROUP + 2 * (1 - child)
    half = skeleton // 2
    theirs = jnp.concatenate([got[beside + at, rhs:, :half] for at in range(2)], axis=1)
    lower = jnp.where(child == 0, mine, theirs)
    higher = jnp.where(child == 0, theirs, mine)
    joined = jnp.concatenate([lower, higher], axis=1)
    v1 = listed(1, target_side(mine, spread))
    aim = target_side(
        dot(joined, one_hot(upper[0, 1:2], 2 * skeleton, 0)).astype(BF16), spread
    )
    tops = got.shape[0] // GROUP
    top = me // GROUP
    gap = jnp.maximum(top - 1, 0)
    width = top + 2 - gap
    batch = min(tops - 2, TOPS)

    def some_tops(step, total):
        nodes = []
        for at in range(batch):
            place = step * batch + at
            k = place + jnp.where(place < gap, 0, width)
            nodes.append((k < tops, *node(jnp.minimum(k, tops - 1) * GROUP, GROUP)))
        return total + potential(aim, nodes)

    v2 = jnp.zeros((rhs, skeleton), F32)
    if tops - 2 == batch:
        v2 = some_tops(0, v2)
    else:
        v2 = lax.fori_loop(0, (tops - 2 + batch - 1) // batch, some_tops, v2)
    for load in loads:
        load.wait()
    z1 = v1 + dot_nt(v2.astype(BF16), ubasis[1])
    z0 = v0 + dot_nt(z1.astype(BF16), ubasis[0])
    z0 = z0.astype(BF16)
    part = near.shape[1] // CUTS
    copies = []
    for at in range(CUTS):
        cut = slice(at * part, (at + 1) * part)
        done[:, cut] = near[:, cut] + dot_nt(z0, basis[cut])
        lane = pl.ds(at * part, part)
        copy = pltpu.make_async_copy(done.at[:, lane], out.at[:, lane], out_sems.at[at])
        copy.start()
        copies.append(copy)
    for copy in copies:
        copy.wait()


def call(kernel, name, out, specs, scratch, flops, alias={}, outs=None, moved=1 << 20):
    return pl.pallas_call(
        kernel,
        out_shape=out,
        in_specs=specs,
        out_specs=jax.tree.map(lambda _: VMEM, out) if outs is None else outs,
        scratch_shapes=scratch,
        compiler_params=pltpu.CompilerParams(vmem_limit_bytes=LIMIT),
        cost_estimate=pl.CostEstimate(flops=flops, bytes_accessed=moved, transcendentals=0),
        input_output_aliases=alias,
        name=name,
    )


def per_device(
    points, charges, near_list, near_count, skel_index, basis, upper_index, upper_basis, far_list
):
    devices = lax.axis_size("leaf")
    rows, feats = points.shape
    rhs = charges.shape[1]
    skeleton = skel_index.shape[1]
    leaves = rows // LEAF
    depth = 128
    pts = points.T
    w = charges.T
    mates = [(i, i ^ 1) for i in range(devices)]
    bridge = [(i, i + 1) for i in range(1, devices - 1, 2)]
    bridge = bridge + [(b, a) for a, b in bridge]
    packed = jnp.concatenate([pts, w], axis=0)
    mate = lax.ppermute(packed, "leaf", mates)
    other = lax.ppermute(packed, "leaf", bridge)
    height = rhs + feats
    levels, own = call(
        points_kernel,
        "points",
        (
            jax.ShapeDtypeStruct((3, feats, skeleton), BF16),
            jax.ShapeDtypeStruct((feats, skeleton), BF16),
        ),
        [VMEM] * 3,
        [],
        int(1e9),
        moved=16 << 20,
    )(pts, skel_index, upper_index)
    sent = call(
        weights_kernel,
        "weights",
        jax.ShapeDtypeStruct((devices, height, skeleton), BF16),
        [VMEM] * 5,
        [pltpu.VMEM((3, height, skeleton), BF16)],
        int(1e9),
    )(w, basis, upper_index, upper_basis, levels)
    got = lax.all_to_all(sent, "leaf", 0, 0)
    todo = pltpu.SMEM((leaves * (near_list.shape[1] + 1) + UNROLL + 1,), jnp.int32)
    whole = pl.BlockSpec(memory_space=pl.ANY)
    field = jax.ShapeDtypeStruct((rhs, rows), F32)
    near = call(
        inside_kernel,
        "near_inside",
        field,
        [SMEM, SMEM, whole, whole],
        [
            pltpu.VMEM(packed.shape, BF16),
            pltpu.VMEM(packed.shape, BF16),
            pltpu.VMEM((leaves + 1, depth, LEAF), BF16),
            pltpu.VMEM((2 * leaves, LEAF, depth), BF16),
            pltpu.VMEM((2 * leaves, rhs, LEAF), BF16),
            pltpu.VMEM((leaves + 1, rhs, LEAF), F32),
            todo,
            todo,
            pltpu.SemaphoreType.DMA((2,)),
        ],
        int(8e9),
    )(near_list, near_count, packed, mate)
    near = call(
        outside_kernel,
        "near_outside",
        field,
        [SMEM, SMEM, VMEM, whole, whole],
        [
            pltpu.VMEM(packed.shape, BF16),
            pltpu.VMEM((rhs, rows), F32),
            pltpu.VMEM((leaves + 1, depth, LEAF), BF16),
            pltpu.VMEM((leaves, LEAF, depth), BF16),
            pltpu.VMEM((leaves, rhs, LEAF), BF16),
            pltpu.VMEM((leaves + 1, rhs, LEAF), F32),
            todo,
            pltpu.SemaphoreType.DMA((2,)),
        ],
        int(8e9),
    )(near_list, near_count, packed, other, near)
    field = call(
        downward_kernel,
        "downward",
        field,
        [SMEM, VMEM, VMEM, VMEM, whole, whole, whole],
        [
            pltpu.VMEM((2, skeleton, skeleton), BF16),
            pltpu.VMEM(basis.shape, BF16),
            pltpu.VMEM((rhs, rows), F32),
            pltpu.VMEM((rhs, rows), F32),
            pltpu.SemaphoreType.DMA((4,)),
            pltpu.SemaphoreType.DMA((CUTS,)),
        ],
        int(1e11),
        {6: 0},
        outs=whole,
        moved=0,
    )(far_list, got, own, upper_index, upper_basis, basis, near)
    return field.T


def solution(mesh):
    both = ("clips", "leaf")
    in_specs = (
        P(both, None),
        P(both, None),
        P(both, None),
        P(both),
        P(both, None),
        P(both, None),
        P(both, None, None),
        P(both, None, None, None),
        P(both, None, None),
    )
    return jax.shard_map(
        per_device, mesh=mesh, in_specs=in_specs, out_specs=P(both, None), check_vma=False
    )
```

```python
import jax
import jax.numpy as jnp
from jax import lax
from jax.experimental import pallas as pl
from jax.experimental.pallas import tpu as pltpu
from jax.sharding import PartitionSpec as P

LEAF = 512
GROUP = 4
UNROLL = 4
CUTS = 4
CODE = 32
TOPS = 2
EXTRA = 16
VMEM = pl.BlockSpec(memory_space=pltpu.VMEM)
SMEM = pl.BlockSpec(memory_space=pltpu.SMEM)
LIMIT = 28 << 20
F32 = jnp.float32
BF16 = jnp.bfloat16


def dot(left, right):
    return jnp.dot(left, right, preferred_element_type=F32)


def dot_nt(left, right):
    return lax.dot_general(left, right, (((1,), (1,)), ((), ())), preferred_element_type=F32)


def dot_tn(left, right):
    return lax.dot_general(left, right, (((0,), (0,)), ((), ())), preferred_element_type=F32)


def norm_rows(feats, spread, ones_first):
    norm = jnp.sum(feats * feats, axis=0, keepdims=True) * (-1.0 / spread)
    high = norm.astype(BF16).astype(F32)
    mid = (norm - high).astype(BF16).astype(F32)
    low = norm - high - mid
    row = lax.broadcasted_iota(jnp.int32, (EXTRA, feats.shape[1]), 0)
    start = 3 if ones_first else 0
    rows = jnp.where((row >= 3 - start) & (row < 6 - start), 1.0, 0.0)
    for at, piece in enumerate((high, mid, low)):
        rows = jnp.where(row == start + at, piece, rows)
    return rows.astype(BF16)


def source_side(feats, spread):
    return jnp.concatenate([feats, norm_rows(feats.astype(F32), spread, False)], axis=0)


def target_side(feats, spread):
    feats_f = feats.astype(F32)
    scaled = (feats_f * (2.0 / spread)).astype(BF16)
    return jnp.concatenate([scaled, norm_rows(feats_f, spread, True)], axis=0)


def padded(rows, height):
    gap = height - rows.shape[0]
    return jnp.concatenate([rows, jnp.zeros((gap, rows.shape[1]), rows.dtype)], axis=0)


def one_hot(index, height, offset):
    rows = lax.broadcasted_iota(jnp.int32, (height, index.shape[1]), 0) + offset
    return jnp.where(rows == index, 1.0, 0.0).astype(BF16)


def chosen_first(upper, side, skeleton):
    half = skeleton // 2
    kept = upper[0, 0:1, pl.ds(pl.multiple_of(side * half, half), half)] - side * skeleton
    pair = lax.broadcasted_iota(jnp.int32, kept.shape, 1)
    order = jnp.concatenate([kept, 4 * pair + 1 - kept], axis=1)
    return one_hot(order, skeleton, 0)


def points_kernel(pts, skel, upper, out, own):
    me = lax.axis_index("leaf")
    side = lax.rem(me, 2)
    child = lax.rem(me // 2, 2)
    rows = pts.shape[1]
    skeleton = own.shape[1]
    half = rows // 2
    lanes = skeleton // 2
    picks = [
        dot(
            pts[:, at * half : (at + 1) * half],
            one_hot(skel[:, at * lanes : (at + 1) * lanes], half, at * half),
        )
        for at in range(2)
    ]
    pts0 = jnp.concatenate(picks, axis=1).astype(BF16)
    own[...] = pts0
    out[0] = dot(pts0, chosen_first(upper, side, skeleton)).astype(BF16)
    pts1 = dot(pts0, one_hot(upper[0, 0:1], skeleton, side * skeleton)).astype(BF16)
    out[1] = pts1
    out[2] = dot(pts1, one_hot(upper[0, 1:2], skeleton, child * skeleton)).astype(BF16)


def weights_kernel(w, basis, upper, ubasis, points, out, block):
    me = lax.axis_index("leaf")
    side = lax.rem(me, 2)
    child = lax.rem(me // 2, 2)
    rhs = w.shape[0]
    skeleton = basis.shape[1]
    w0 = dot(w[...], basis[...]).astype(BF16)
    low = pl.multiple_of(side * skeleton, skeleton)
    w1 = dot(w0, ubasis[0, 0, pl.ds(low, skeleton), :]).astype(BF16)
    up = pl.multiple_of(child * skeleton, skeleton)
    w2 = dot(w1, ubasis[0, 1, pl.ds(up, skeleton), :]).astype(BF16)
    block[0, 0:rhs] = dot(w0, chosen_first(upper, side, skeleton)).astype(BF16)
    block[1, 0:rhs] = w1
    block[2, 0:rhs] = w2
    block[:, rhs:] = points[...]

    def send(to, carry):
        near = jnp.abs(to // 2 - me // 2) == 1
        away = jnp.abs(to // GROUP - me // GROUP) >= 2
        out[to] = block[jnp.where(near, 0, jnp.where(away, 2, 1))]
        return carry

    lax.fori_loop(0, out.shape[0], send, 0)


def note_pairs(near, count, first, leaves, lists, starts):
    ends = tuple(jnp.int32(start) for start in starts)
    for leaf in range(leaves):

        def note(slot, ends, leaf=leaf):
            b = near[leaf, slot] - first
            after = []
            for end, (to, wanted) in zip(ends, lists):
                keep, place = wanted(leaf, b)
                to[end] = place + leaf * CODE
                after.append(end + keep.astype(jnp.int32))
            return tuple(after)

        ends = lax.fori_loop(0, count[leaf], note, ends)
    for end, (to, _) in zip(ends, lists):
        for at in range(UNROLL):
            to[end + at] = leaves * CODE
    return ends


def over_pairs(todo, length, unroll, work):
    def decoded(start, span):
        codes = [todo[start + at] for at in range(span)]
        return [(code // CODE, lax.rem(code, CODE)) for code in codes]

    def step(at, carry):
        work(decoded(at * unroll, unroll))
        return carry

    rounds = (length + 1) // unroll
    lax.fori_loop(0, rounds, step, 0)
    done = rounds * unroll
    span = unroll // 2
    while span >= 2:
        fits = length - done > span - 2

        @pl.when(fits)
        def _(done=done, span=span):
            work(decoded(done, span))

        done = done + jnp.where(fits, span, 0)
        span //= 2


def halo_place(b, leaves, held):
    return jnp.where(b < 0, b + held, jnp.maximum(b - leaves, 0))


def inside_kernel(
    near, count, held, mate_in, out, mate, target, source, weights, acc, pairs, singles, sems
):
    rhs = weights.shape[1]
    feats, rows = held.shape[0] - rhs, held.shape[1]
    leaves = rows // LEAF
    spread = 0.5 * feats
    moves = ((mate_in, mate),)
    loads = [pltpu.make_async_copy(a, b, sems.at[at]) for at, (a, b) in enumerate(moves)]
    for load in loads:
        load.start()
    me = lax.axis_index("leaf")
    even = lax.rem(me, 2) == 0
    for leaf in range(leaves):
        singles[leaf] = leaf * CODE + leaf
    lengths = note_pairs(
        near, count, me * leaves, leaves,
        (
            (pairs, lambda a, b: ((b > a) & (b < leaves), jnp.clip(b, 0, leaves - 1))),
            (
                singles,
                lambda a, b: (
                    ((b < 0) != even) & ((b < 0) | (b >= leaves)),
                    halo_place(b, leaves, leaves) + leaves,
                ),
            ),
        ),
        (0, leaves),
    )
    acc[...] = jnp.zeros_like(acc)
    target[leaves] = jnp.zeros_like(target[leaves])
    for leaf in range(leaves):
        at = slice(leaf * LEAF, (leaf + 1) * LEAF)
        source[leaf] = padded(source_side(held[:feats, at], spread), source.shape[2]).T
        target[leaf] = padded(target_side(held[:feats, at], spread), target.shape[1])
        weights[leaf] = held[feats:, at]

    def tile(a, b):
        return jnp.exp(dot(source[b], target[a])).astype(BF16)

    def single(these):
        tiles = [tile(a, b) for a, b in these]
        for (a, b), t in zip(these, tiles):
            acc[a] += dot(weights[b], t)

    def pair(these):
        tiles = [tile(a, b) for a, b in these]
        for (a, b), t in zip(these, tiles):
            acc[a] += dot(weights[b], t)
            acc[b] += dot_nt(weights[a], t)

    weights[leaves] = jnp.zeros_like(weights[0])
    over_pairs(pairs, lengths[0], 2 * UNROLL, pair)
    loads[0].wait()
    for leaf in range(leaves):
        at = slice(leaf * LEAF, (leaf + 1) * LEAF)
        source[leaves + leaf] = padded(source_side(mate[:feats, at], spread), source.shape[2]).T
        weights[leaves + leaf] = mate[feats:, at]
    over_pairs(singles, lengths[1], 4 * UNROLL, single)
    for leaf in range(leaves):
        out[:, leaf * LEAF : (leaf + 1) * LEAF] = acc[leaf]


def outside_kernel(
    near, count, held, other_in, inside_in, out,
    other, inside, target, source, weights, acc, singles, sems,
):
    rhs, rows = inside.shape
    feats = held.shape[0] - rhs
    leaves = rows // LEAF
    spread = 0.5 * feats
    middle = rows // 2
    moves = [(inside_in, inside)]
    for at in range(2):
        lane = pl.ds(at * middle, middle)
        moves.append((other_in.at[:, lane], other.at[:, lane]))
    loads = [pltpu.make_async_copy(a, b, sems.at[at]) for at, (a, b) in enumerate(moves)]
    for load in loads:
        load.start()
    me = lax.axis_index("leaf")
    even = lax.rem(me, 2) == 0
    lengths = note_pairs(
        near, count, me * leaves, leaves,
        (
            (
                singles,
                lambda a, b: (
                    ((b < 0) == even) & ((b < 0) | (b >= leaves)),
                    halo_place(b, leaves, leaves),
                ),
            ),
        ),
        (0,),
    )
    acc[leaves] = jnp.zeros_like(acc[leaves])
    target[leaves] = jnp.zeros_like(target[leaves])
    loads[0].wait()
    for leaf in range(leaves):
        at = slice(leaf * LEAF, (leaf + 1) * LEAF)
        target[leaf] = padded(target_side(held[:feats, at], spread), target.shape[1])
        acc[leaf] = inside[:, at]
    for leaf in range(leaves):
        at = slice(leaf * LEAF, (leaf + 1) * LEAF)
        if leaf % (leaves // 2) == 0:
            loads[1 + leaf // (leaves // 2)].wait()
        source[leaf] = padded(source_side(other[:feats, at], spread), source.shape[2]).T
        weights[leaf] = other[feats:, at]

    def single(these):
        tiles = [jnp.exp(dot(source[b], target[a])).astype(BF16) for a, b in these]
        for (a, b), t in zip(these, tiles):
            acc[a] += dot(weights[b], t)

    over_pairs(singles, lengths[0], 2 * UNROLL, single)
    for leaf in range(leaves):
        out[:, leaf * LEAF : (leaf + 1) * LEAF] = acc[leaf]


def downward_kernel(
    far, got, own, upper, ubasis_in, basis_in, near_in, out,
    ubasis, basis, near, done, in_sems, out_sems,
):
    me = lax.axis_index("leaf")
    side = lax.rem(me, 2)
    child = lax.rem(me // 2, 2)
    feats, skeleton = own.shape
    rhs = near.shape[0]
    halves = [pl.ds(pl.multiple_of(at * skeleton, skeleton), skeleton) for at in (side, child)]
    moves = [
        (ubasis_in.at[0, 1, halves[1]], ubasis.at[1]),
        (ubasis_in.at[0, 0, halves[0]], ubasis.at[0]),
        (near_in, near),
        (basis_in, basis),
    ]
    loads = [pltpu.make_async_copy(a, b, in_sems.at[at]) for at, (a, b) in enumerate(moves)]
    for load in loads:
        load.start()
    spread = 0.5 * feats
    slots = far.shape[2]

    def node(start, span):
        parts = got[start].astype(F32)
        for at in range(1, span):
            parts = parts + got[start + at].astype(F32)
        return parts[0:rhs], parts[rhs : rhs + feats].astype(BF16)

    def potential(aim, nodes):
        weights = [jnp.where(counts, w, 0.0).astype(BF16) for counts, w, _ in nodes]
        points = jnp.concatenate([p for _, _, p in nodes], axis=1)
        tile = jnp.exp(dot_tn(aim, source_side(points, spread))).astype(BF16)
        return dot_nt(jnp.concatenate(weights, axis=1), tile)

    def listed(level, aim):
        nodes = []
        for slot in range(slots):
            k = far[0, level, slot]
            nodes.append((k >= 0, *node(jnp.maximum(k, 0) * 2**level, 2**level)))
        return potential(aim, nodes)

    v0 = listed(0, target_side(own[...], spread))
    mine = node(me // 2 * 2, 2)[1]
    beside = me // GROUP * GROUP + 2 * (1 - child)
    half = skeleton // 2
    theirs = jnp.concatenate([got[beside + at, rhs:, :half] for at in range(2)], axis=1)
    lower = jnp.where(child == 0, mine, theirs)
    higher = jnp.where(child == 0, theirs, mine)
    joined = jnp.concatenate([lower, higher], axis=1)
    v1 = listed(1, target_side(mine, spread))
    aim = target_side(
        dot(joined, one_hot(upper[0, 1:2], 2 * skeleton, 0)).astype(BF16), spread
    )
    tops = got.shape[0] // GROUP
    top = me // GROUP
    gap = jnp.maximum(top - 1, 0)
    width = top + 2 - gap
    batch = min(tops - 2, TOPS)

    def some_tops(step, total):
        nodes = []
        for at in range(batch):
            place = step * batch + at
            k = place + jnp.where(place < gap, 0, width)
            nodes.append((k < tops, *node(jnp.minimum(k, tops - 1) * GROUP, GROUP)))
        return total + potential(aim, nodes)

    v2 = jnp.zeros((rhs, skeleton), F32)
    if tops - 2 == batch:
        v2 = some_tops(0, v2)
    else:
        v2 = lax.fori_loop(0, (tops - 2 + batch - 1) // batch, some_tops, v2)
    for load in loads:
        load.wait()
    z1 = v1 + dot_nt(v2.astype(BF16), ubasis[1])
    z0 = v0 + dot_nt(z1.astype(BF16), ubasis[0])
    z0 = z0.astype(BF16)
    part = near.shape[1] // CUTS
    copies = []
    for at in range(CUTS):
        cut = slice(at * part, (at + 1) * part)
        done[:, cut] = near[:, cut] + dot_nt(z0, basis[cut])
        lane = pl.ds(at * part, part)
        copy = pltpu.make_async_copy(done.at[:, lane], out.at[:, lane], out_sems.at[at])
        copy.start()
        copies.append(copy)
    for copy in copies:
        copy.wait()


def call(kernel, name, out, specs, scratch, flops, alias={}, outs=None, moved=1 << 20):
    return pl.pallas_call(
        kernel,
        out_shape=out,
        in_specs=specs,
        out_specs=jax.tree.map(lambda _: VMEM, out) if outs is None else outs,
        scratch_shapes=scratch,
        compiler_params=pltpu.CompilerParams(vmem_limit_bytes=LIMIT),
        cost_estimate=pl.CostEstimate(flops=flops, bytes_accessed=moved, transcendentals=0),
        input_output_aliases=alias,
        name=name,
    )


def per_device(
    points, charges, near_list, near_count, skel_index, basis, upper_index, upper_basis, far_list
):
    devices = lax.axis_size("leaf")
    rows, feats = points.shape
    rhs = charges.shape[1]
    skeleton = skel_index.shape[1]
    leaves = rows // LEAF
    depth = 128
    pts = points.T
    w = charges.T
    mates = [(i, i ^ 1) for i in range(devices)]
    bridge = [(i, i + 1) for i in range(1, devices - 1, 2)]
    bridge = bridge + [(b, a) for a, b in bridge]
    packed = jnp.concatenate([pts, w], axis=0)
    mate = lax.ppermute(packed, "leaf", mates)
    other = lax.ppermute(packed, "leaf", bridge)
    height = rhs + feats
    levels, own = call(
        points_kernel,
        "points",
        (
            jax.ShapeDtypeStruct((3, feats, skeleton), BF16),
            jax.ShapeDtypeStruct((feats, skeleton), BF16),
        ),
        [VMEM] * 3,
        [],
        int(1e9),
        moved=16 << 20,
    )(pts, skel_index, upper_index)
    sent = call(
        weights_kernel,
        "weights",
        jax.ShapeDtypeStruct((devices, height, skeleton), BF16),
        [VMEM] * 5,
        [pltpu.VMEM((3, height, skeleton), BF16)],
        int(1e9),
    )(w, basis, upper_index, upper_basis, levels)
    got = lax.all_to_all(sent, "leaf", 0, 0)
    todo = pltpu.SMEM((leaves * (near_list.shape[1] + 1) + UNROLL + 1,), jnp.int32)
    whole = pl.BlockSpec(memory_space=pl.ANY)
    field = jax.ShapeDtypeStruct((rhs, rows), F32)
    near = call(
        inside_kernel,
        "near_inside",
        field,
        [SMEM, SMEM, VMEM, whole],
        [
            pltpu.VMEM(packed.shape, BF16),
            pltpu.VMEM((leaves + 1, depth, LEAF), BF16),
            pltpu.VMEM((2 * leaves, LEAF, depth), BF16),
            pltpu.VMEM((2 * leaves, rhs, LEAF), BF16),
            pltpu.VMEM((leaves + 1, rhs, LEAF), F32),
            todo,
            todo,
            pltpu.SemaphoreType.DMA((1,)),
        ],
        int(8e9),
    )(near_list, near_count, packed, mate)
    near = call(
        outside_kernel,
        "near_outside",
        field,
        [SMEM, SMEM, VMEM, whole, whole],
        [
            pltpu.VMEM(packed.shape, BF16),
            pltpu.VMEM((rhs, rows), F32),
            pltpu.VMEM((leaves + 1, depth, LEAF), BF16),
            pltpu.VMEM((leaves, LEAF, depth), BF16),
            pltpu.VMEM((leaves, rhs, LEAF), BF16),
            pltpu.VMEM((leaves + 1, rhs, LEAF), F32),
            todo,
            pltpu.SemaphoreType.DMA((3,)),
        ],
        int(8e9),
    )(near_list, near_count, packed, other, near)
    field = call(
        downward_kernel,
        "downward",
        field,
        [SMEM, VMEM, VMEM, VMEM, whole, whole, whole],
        [
            pltpu.VMEM((2, skeleton, skeleton), BF16),
            pltpu.VMEM(basis.shape, BF16),
            pltpu.VMEM((rhs, rows), F32),
            pltpu.VMEM((rhs, rows), F32),
            pltpu.SemaphoreType.DMA((4,)),
            pltpu.SemaphoreType.DMA((CUTS,)),
        ],
        int(1e11),
        {6: 0},
        outs=whole,
        moved=0,
    )(far_list, got, own, upper_index, upper_basis, basis, near)
    return field.T


def solution(mesh):
    both = ("clips", "leaf")
    in_specs = (
        P(both, None),
        P(both, None),
        P(both, None),
        P(both),
        P(both, None),
        P(both, None),
        P(both, None, None),
        P(both, None, None, None),
        P(both, None, None),
    )
    return jax.shard_map(
        per_device, mesh=mesh, in_specs=in_specs, out_specs=P(both, None), check_vma=False
    )
```
